512 devices in a mesh: context: 64 (over y, z), tensor: 8 (over x, core).
Axes of the slice: x: 4, y: 8, z: 8, core: 2. Of those that a mesh axis runs over, the one named last changes fastest.
Arguments:
- queries: bfloat16 [8192, 4096], P('context', 'tensor'), may hold values from -6 to 6
- key_gate: bfloat16 [8192, 4096], P('context', 'tensor'), may hold values from -6 to 6
- values: bfloat16 [8192, 4096], P('context', 'tensor'), may hold values from -6 to 6
- residues: float32 [16, 4096], P(None, 'tensor'), may hold values from -0.0625 to 0.0625
- decay_rates: float32 [16, 4096], P(None, 'tensor'), may hold values from 1 to 256
- out_weight: bfloat16 [4096, 4096], P('tensor'), may hold values from -0.09375 to 0.09375
Outputs:
- mixed_rows: bfloat16 [8192, 4096], P('context', 'tensor')
The draws below stay inside these ranges and needn't reach their ends.
All inputs are finite; a program needn't handle non-finite values.
Results may differ from the reference program's by a relative error of at most 0.024.
Values may be sent and summed in bfloat16 or wider, within the bound.
No kernel may reach another device: no remote copies, remote signals or barrier semaphores. Data moves between devices by JAX's collectives and lax.ppermute only.
A program may use at most 64 MiB of HBM per device.

```python
import math
import jax
import jax.numpy as jnp
from jax import lax

D = 4096
POLES = 16
SEQ = 8192
N_TENSOR = 8


def level_of(rng, shape, shards, least, largest):
    gain, own = 1.0, jax.random.fold_in(rng, 6)
    for dim, blocks in shards:
        draws = jnp.exp(jax.random.uniform(jax.random.fold_in(own, dim), (blocks,), jnp.float32, least / len(shards), largest / len(shards)))
        gain = gain * jnp.repeat(draws, shape[dim] // blocks).reshape([-1 if axis == dim else 1 for axis in range(len(shape))])
    return gain


def gaussian(stream_key, extent, spread, most, cuts=(), kind=jnp.bfloat16):
    loudness = level_of(stream_key, extent, cuts, -0.22, 0.18) if cuts else 1.0
    result = jax.random.normal(stream_key, extent, jnp.float32) * spread * loudness
    return jnp.minimum(jnp.maximum(result, -most), most).astype(kind)


def setup_inputs(seed: int = 0) -> dict:
    key_list = jax.random.split(jax.random.key(seed), 7)
    return {
        "queries": gaussian(key_list[0], (SEQ, D), 1.0, 6.0, ((0, 64), (1, 8))),
        "key_gate": gaussian(key_list[1], (SEQ, D), 1.0, 6.0, ((0, 64), (1, 8))),
        "values": gaussian(key_list[2], (SEQ, D), 1.0, 6.0, ((0, 64), (1, 8))),
        "residues": gaussian(key_list[3], (POLES, D), SEQ ** -0.5, 0.0625, ((1, 8),), jnp.float32),
        "decay_rates": jnp.clip(jnp.exp(math.log(256.0) - 5.5451774 * jax.random.uniform(key_list[4], (POLES, D), jnp.float32) ** level_of(key_list[4], (POLES, D), ((1, 8),), -0.2, 0.2)), 1.0, 256.0),
        "out_weight": gaussian(key_list[5], (D, D), D ** -0.5, 0.09375, ((0, 8),)),
    }


def causal_block(residue_cols, rate_cols, signal):
    positions = jnp.arange(SEQ, dtype=jnp.float32)[:, None]
    filter_rows = jnp.zeros(signal.shape, jnp.float32)
    for pole_index in range(POLES):
        filter_rows = filter_rows + residue_cols[pole_index][None, :] * jnp.exp(-rate_cols[pole_index][None, :] * positions / SEQ)
    fft_length = 2 * SEQ
    spectrum = jnp.fft.rfft(filter_rows, n=fft_length, axis=0) * jnp.fft.rfft(signal, n=fft_length, axis=0)
    return jnp.fft.irfft(spectrum, n=fft_length, axis=0)[:SEQ]


def reference(queries, key_gate, values, residues, decay_rates, out_weight):
    product = (key_gate.astype(jnp.float32) * values.astype(jnp.float32)).astype(jnp.bfloat16)
    signal = lax.optimization_barrier(product).astype(jnp.float32)
    block_width = min(D, 512)
    pieces = []
    for first_col in range(0, D, block_width):
        last_col = first_col + block_width
        pieces.append(causal_block(residues[:, first_col:last_col], decay_rates[:, first_col:last_col], signal[:, first_col:last_col]))
    convolved = jnp.concatenate(pieces, axis=1)
    gated_rows = (queries.astype(jnp.float32) * convolved).astype(jnp.bfloat16)
    group_rows = D // N_TENSOR
    summed = jnp.zeros((SEQ, D), jnp.float32)
    for group_index in range(N_TENSOR):
        first_row = group_index * group_rows
        partial_value = jnp.dot(gated_rows[:, first_row:first_row + group_rows], out_weight[first_row:first_row + group_rows], preferred_element_type=jnp.float32)
        rounded = lax.optimization_barrier(partial_value.astype(jnp.bfloat16))
        summed = summed + rounded.astype(jnp.float32)
    return summed.astype(jnp.bfloat16)
```

```python
import jax
import jax.numpy as jnp
from jax import lax
from jax.experimental import pallas as pl
from jax.experimental.pallas import tpu as pltpu
from jax.sharding import PartitionSpec as P

SEQ = 8192
POLES = 16
ROWS = 128
CHANNELS = 512
LANES = 128
SUBS = 8
STEPS = ROWS // SUBS
RING = 8
XCHIPS = 4
LINK = jnp.bfloat16

GROUPS = tuple(slice(g * LANES, (g + 1) * LANES) for g in range(CHANNELS // LANES))
Z_GROUPS = [[y * RING + z for z in range(RING)] for y in range(RING)]
Y_GROUPS = [[y * RING + z for y in range(RING)] for z in range(RING)]
X_GROUPS = [[x * 2 + core for x in range(XCHIPS)] for core in range(2)]
SIBLING = [(t, t ^ 1) for t in range(2 * XCHIPS)]


def over_subs(rows):
    return jnp.broadcast_to(rows[:, None, :], (POLES, SUBS, LANES))


def sub_index():
    return lax.broadcasted_iota(jnp.int32, (POLES, SUBS, LANES), 1).astype(jnp.float32)


def end_states(gate_ref, value_ref, rate_ref, x_ref, ends_ref, send_ref):
    product = gate_ref[...].astype(jnp.float32) * value_ref[...].astype(jnp.float32)
    product = product.astype(jnp.bfloat16).astype(jnp.float32)
    for g, lanes in enumerate(GROUPS):
        x_ref[g] = product[:, lanes]
        rate = rate_ref[:, lanes] / SEQ
        shrink = over_subs(jnp.exp(-rate))
        state = jnp.zeros((POLES, SUBS, LANES), jnp.float32)
        for t in range(STEPS):
            row = x_ref[g, pl.ds(t, SUBS, stride=STEPS), :]
            state = shrink * state + row[None]
        ends_ref[:, :, lanes] = state
        left = STEPS * (SUBS - 1.0 - sub_index())
        total = jnp.sum(state * jnp.exp(-over_subs(rate) * left), axis=1).astype(LINK)
        for j in range(RING):
            send_ref[j, :, lanes] = total


def chunk_carry(came_ref, rate_ref, prior_ref, send_ref):
    z = lax.rem(lax.axis_index("context"), RING)
    shrink = jnp.exp(-rate_ref[...] * (ROWS / SEQ))
    prior = jnp.zeros((POLES, CHANNELS), jnp.float32)
    total = jnp.zeros((POLES, CHANNELS), jnp.float32)
    for j in range(RING):
        came = came_ref[j].astype(jnp.float32)
        prior = jnp.where(j < z, prior * shrink + came, prior)
        total = total * shrink + came
    prior_ref[...] = prior
    sent = total.astype(LINK)
    for j in range(RING):
        send_ref[j] = sent


def convolve_project(
    came_ref, prior_ref, ends_ref, x_ref, query_ref, residue_ref, rate_ref, weight_ref,
    keep_ref, send_ref, y_ref,
):
    context = lax.axis_index("context")
    core = lax.rem(lax.axis_index("tensor"), 2)
    z, y = lax.rem(context, RING), context // RING
    shrink = jnp.exp(-rate_ref[...] * (RING * ROWS / SEQ))
    carry = jnp.zeros((POLES, CHANNELS), jnp.float32)
    for j in range(RING):
        carry = jnp.where(j < y, carry * shrink + came_ref[j].astype(jnp.float32), carry)
    behind = (z * ROWS).astype(jnp.float32) / SEQ
    carry = carry * jnp.exp(-rate_ref[...] * behind) + prior_ref[...]
    for g, lanes in enumerate(GROUPS):
        rate = rate_ref[:, lanes] / SEQ
        steps = over_subs(rate)
        shrink_sub = jnp.exp(-steps * STEPS)
        sub = sub_index()
        state = jnp.where(sub > 0, pltpu.roll(ends_ref[:, :, lanes], 1, 1), over_subs(carry[:, lanes]))
        for shift in (1, 2, 4):
            state = state + jnp.where(sub >= shift, pltpu.roll(state, shift, 1), 0.0) * shrink_sub
            shrink_sub = shrink_sub * shrink_sub
        shrink_one = over_subs(jnp.exp(-rate))
        residue = over_subs(residue_ref[:, lanes])
        for t in range(STEPS):
            row = x_ref[g, pl.ds(t, SUBS, stride=STEPS), :]
            state = shrink_one * state + row[None]
            y_ref[g, pl.ds(t, SUBS, stride=STEPS), :] = jnp.sum(residue * state, axis=0)
    convolved = jnp.concatenate([y_ref[g] for g in range(len(GROUPS))], axis=1)
    gated = (query_ref[...].astype(jnp.float32) * convolved).astype(jnp.bfloat16)
    for out_ref, owner in ((send_ref, 1 - core), (keep_ref, core)):
        for chip in range(XCHIPS):
            column = pl.multiple_of((2 * chip + owner) * CHANNELS, CHANNELS)
            partial = jnp.dot(
                gated, weight_ref[:, pl.ds(column, CHANNELS)], preferred_element_type=jnp.float32
            )
            out_ref[chip] = partial.astype(out_ref.dtype)


def add_pair(kept_ref, came_ref, out_ref):
    total = kept_ref[...].astype(jnp.float32) + came_ref[...].astype(jnp.float32)
    out_ref[...] = total.astype(out_ref.dtype)


def add_chips(came_ref, out_ref):
    total = came_ref[0].astype(jnp.float32)
    for chip in range(1, XCHIPS):
        total = total + came_ref[chip].astype(jnp.float32)
    out_ref[...] = total.astype(out_ref.dtype)


def kernel(body, outs, scratch=(), flops=0, moved=0):
    return pl.pallas_call(
        body,
        out_shape=[jax.ShapeDtypeStruct(shape, dtype) for shape, dtype in outs],
        scratch_shapes=scratch,
        compiler_params=pltpu.CompilerParams(vmem_limit_bytes=32 * 2**20),
        cost_estimate=pl.CostEstimate(flops=flops, bytes_accessed=moved, transcendentals=0),
    )


def on_device(queries, key_gate, values, residues, decay_rates, out_weight):
    f32, bf16 = jnp.float32, jnp.bfloat16
    block = (RING, POLES, CHANNELS)
    x, ends, sent = kernel(
        end_states,
        [((len(GROUPS), ROWS, LANES), f32), ((POLES, SUBS, CHANNELS), f32), (block, LINK)],
        flops=8_000_000, moved=1_000_000,
    )(key_gate, values, decay_rates)
    came = lax.all_to_all(sent, "context", 0, 0, axis_index_groups=Z_GROUPS)
    prior, sent = kernel(
        chunk_carry, [((POLES, CHANNELS), f32), (block, LINK)], flops=500_000, moved=300_000
    )(came, decay_rates)
    came = lax.all_to_all(sent, "context", 0, 0, axis_index_groups=Y_GROUPS)
    halves = (XCHIPS, ROWS, CHANNELS)
    kept, sent = kernel(
        convolve_project,
        [(halves, bf16), (halves, bf16)],
        scratch=[pltpu.VMEM((len(GROUPS), ROWS, LANES), f32)],
        flops=600_000_000, moved=6_000_000,
    )(came, prior, ends, x, queries, residues, decay_rates, out_weight)
    came = lax.ppermute(sent, "tensor", SIBLING)
    (pair,) = kernel(add_pair, [(halves, bf16)], flops=300_000, moved=1_500_000)(kept, came)
    came = lax.all_to_all(pair, "tensor", 0, 0, axis_index_groups=X_GROUPS)
    (mixed,) = kernel(add_chips, [((ROWS, CHANNELS), bf16)], flops=300_000, moved=700_000)(came)
    return mixed


def solution(mesh):
    in_specs = (
        P("context", "tensor"),
        P("context", "tensor"),
        P("context", "tensor"),
        P(None, "tensor"),
        P(None, "tensor"),
        P("tensor", None),
    )
    out_specs = P("context", "tensor")
    return jax.shard_map(
        on_device, mesh=mesh, in_specs=in_specs, out_specs=out_specs, check_vma=False
    )
```

```python
import jax
import jax.numpy as jnp
from jax import lax
from jax.experimental import pallas as pl
from jax.experimental.pallas import tpu as pltpu
from jax.sharding import PartitionSpec as P

SEQ = 8192
POLES = 16
ROWS = 128
CHANNELS = 512
LANES = 128
SUBS = 8
STEPS = ROWS // SUBS
RING = 8
XCHIPS = 4
LINK = jnp.bfloat16

GROUPS = tuple(slice(g * LANES, (g + 1) * LANES) for g in range(CHANNELS // LANES))
Z_GROUPS = [[y * RING + z for z in range(RING)] for y in range(RING)]
Y_GROUPS = [[y * RING + z for y in range(RING)] for z in range(RING)]
X_GROUPS = [[x * 2 + core for x in range(XCHIPS)] for core in range(2)]
SIBLING = [(t, t ^ 1) for t in range(2 * XCHIPS)]


def over_subs(rows):
    return jnp.broadcast_to(rows[:, None, :], (POLES, SUBS, LANES))


def sub_index():
    return lax.broadcasted_iota(jnp.int32, (POLES, SUBS, LANES), 1).astype(jnp.float32)


def end_states(
    gate_hbm, value_hbm, rate_hbm, x_ref, ends_ref, send_ref, gate_ref, value_ref, rate_ref, sems
):
    pairs = ((gate_hbm, gate_ref), (value_hbm, value_ref), (rate_hbm, rate_ref))
    copies = [pltpu.make_async_copy(a, b, sems.at[i]) for i, (a, b) in enumerate(pairs)]
    for copy in copies:
        copy.start()
    for copy in copies:
        copy.wait()
    product = gate_ref[...].astype(jnp.float32) * value_ref[...].astype(jnp.float32)
    product = product.astype(jnp.bfloat16).astype(jnp.float32)
    for g, lanes in enumerate(GROUPS):
        x_ref[g] = product[:, lanes]
        rate = rate_ref[:, lanes] / SEQ
        shrink = over_subs(jnp.exp(-rate))
        state = jnp.zeros((POLES, SUBS, LANES), jnp.float32)
        for t in range(STEPS):
            row = x_ref[g, pl.ds(t, SUBS, stride=STEPS), :]
            state = shrink * state + row[None]
        ends_ref[:, :, lanes] = state
        left = STEPS * (SUBS - 1.0 - sub_index())
        total = jnp.sum(state * jnp.exp(-over_subs(rate) * left), axis=1).astype(LINK)
        for j in range(RING):
            send_ref[j, :, lanes] = total


def chunk_carry(came_ref, rate_ref, prior_ref, send_ref):
    z = lax.rem(lax.axis_index("context"), RING)
    shrink = jnp.exp(-rate_ref[...] * (ROWS / SEQ))
    prior = jnp.zeros((POLES, CHANNELS), jnp.float32)
    total = jnp.zeros((POLES, CHANNELS), jnp.float32)
    for j in range(RING):
        came = came_ref[j].astype(jnp.float32)
        prior = jnp.where(j < z, prior * shrink + came, prior)
        total = total * shrink + came
    prior_ref[...] = prior
    sent = total.astype(LINK)
    for j in range(RING):
        send_ref[j] = sent


def convolve_project(
    came_ref, prior_ref, ends_ref, x_ref, query_ref, residue_ref, rate_ref, weight_ref,
    send_ref, gated_ref, y_ref,
):
    context = lax.axis_index("context")
    core = lax.rem(lax.axis_index("tensor"), 2)
    z, y = lax.rem(context, RING), context // RING
    shrink = jnp.exp(-rate_ref[...] * (RING * ROWS / SEQ))
    carry = jnp.zeros((POLES, CHANNELS), jnp.float32)
    for j in range(RING):
        carry = jnp.where(j < y, carry * shrink + came_ref[j].astype(jnp.float32), carry)
    behind = (z * ROWS).astype(jnp.float32) / SEQ
    carry = carry * jnp.exp(-rate_ref[...] * behind) + prior_ref[...]
    for g, lanes in enumerate(GROUPS):
        rate = rate_ref[:, lanes] / SEQ
        steps = over_subs(rate)
        shrink_sub = jnp.exp(-steps * STEPS)
        sub = sub_index()
        state = jnp.where(sub > 0, pltpu.roll(ends_ref[:, :, lanes], 1, 1), over_subs(carry[:, lanes]))
        for shift in (1, 2, 4):
            state = state + jnp.where(sub >= shift, pltpu.roll(state, shift, 1), 0.0) * shrink_sub
            shrink_sub = shrink_sub * shrink_sub
        shrink_one = over_subs(jnp.exp(-rate))
        residue = over_subs(residue_ref[:, lanes])
        for t in range(STEPS):
            row = x_ref[g, pl.ds(t, SUBS, stride=STEPS), :]
            state = shrink_one * state + row[None]
            y_ref[g, pl.ds(t, SUBS, stride=STEPS), :] = jnp.sum(residue * state, axis=0)
    convolved = jnp.concatenate([y_ref[g] for g in range(len(GROUPS))], axis=1)
    gated = (query_ref[...].astype(jnp.float32) * convolved).astype(jnp.bfloat16)
    gated_ref[...] = gated
    project(gated, weight_ref, 1 - core, send_ref)


def project(gated, weight_ref, core, out_ref):
    for chip in range(XCHIPS):
        column = pl.multiple_of((2 * chip + core) * CHANNELS, CHANNELS)
        partial = jnp.dot(
            gated, weight_ref[:, pl.ds(column, CHANNELS)], preferred_element_type=jnp.float32
        )
        out_ref[chip] = partial.astype(out_ref.dtype)


def project_own(gated_ref, weight_ref, keep_ref):
    project(gated_ref[...], weight_ref, lax.rem(lax.axis_index("tensor"), 2), keep_ref)


def add_pair(kept_ref, came_ref, out_ref):
    total = kept_ref[...].astype(jnp.float32) + came_ref[...].astype(jnp.float32)
    out_ref[...] = total.astype(out_ref.dtype)


def add_chips(came_ref, out_ref):
    total = came_ref[0].astype(jnp.float32)
    for chip in range(1, XCHIPS):
        total = total + came_ref[chip].astype(jnp.float32)
    out_ref[...] = total.astype(out_ref.dtype)


def kernel(body, outs, scratch=(), flops=0, moved=0, **specs):
    return pl.pallas_call(
        body,
        **specs,
        out_shape=[jax.ShapeDtypeStruct(shape, dtype) for shape, dtype in outs],
        scratch_shapes=scratch,
        compiler_params=pltpu.CompilerParams(vmem_limit_bytes=32 * 2**20),
        cost_estimate=pl.CostEstimate(flops=flops, bytes_accessed=moved, transcendentals=0),
    )


def on_device(queries, key_gate, values, residues, decay_rates, out_weight):
    f32, bf16 = jnp.float32, jnp.bfloat16
    block = (RING, POLES, CHANNELS)
    rows, modes = (ROWS, CHANNELS), (POLES, CHANNELS)
    x, ends, sent = kernel(
        end_states,
        [((len(GROUPS), ROWS, LANES), f32), ((POLES, SUBS, CHANNELS), f32), (block, LINK)],
        scratch=[
            pltpu.VMEM(rows, bf16),
            pltpu.VMEM(rows, bf16),
            pltpu.VMEM(modes, f32),
            pltpu.SemaphoreType.DMA((3,)),
        ],
        in_specs=[pl.BlockSpec(memory_space=pltpu.HBM)] * 3,
        flops=8_000_000_000, moved=1_000_000,
    )(*(pltpu.with_memory_space_constraint(a, pltpu.HBM) for a in (key_gate, values, decay_rates)))
    came = lax.all_to_all(sent, "context", 0, 0, axis_index_groups=Z_GROUPS)
    prior, sent = kernel(
        chunk_carry, [(modes, f32), (block, LINK)], flops=8_000_000_000, moved=300_000
    )(came, decay_rates)
    came = lax.all_to_all(sent, "context", 0, 0, axis_index_groups=Y_GROUPS)
    halves = (XCHIPS, ROWS, CHANNELS)
    sent, gated = kernel(
        convolve_project,
        [(halves, bf16), (rows, bf16)],
        scratch=[pltpu.VMEM((len(GROUPS), ROWS, LANES), f32)],
        flops=300_000_000, moved=3_000_000,
    )(came, prior, ends, x, queries, residues, decay_rates, out_weight)
    came = lax.ppermute(sent, "tensor", SIBLING)
    (kept,) = kernel(project_own, [(halves, f32)], flops=600_000_000, moved=3_000_000)(
        gated, out_weight
    )
    (pair,) = kernel(add_pair, [(halves, bf16)], flops=300_000, moved=1_500_000)(kept, came)
    came = lax.all_to_all(pair, "tensor", 0, 0, axis_index_groups=X_GROUPS)
    (mixed,) = kernel(add_chips, [(rows, bf16)], flops=300_000, moved=700_000)(came)
    return mixed


def solution(mesh):
    in_specs = (
        P("context", "tensor"),
        P("context", "tensor"),
        P("context", "tensor"),
        P(None, "tensor"),
        P(None, "tensor"),
        P("tensor", None),
    )
    out_specs = P("context", "tensor")
    return jax.shard_map(
        on_device, mesh=mesh, in_specs=in_specs, out_specs=out_specs, check_vma=False
    )
```

```python
import jax
import jax.numpy as jnp
from jax import lax
from jax.experimental import pallas as pl
from jax.experimental.pallas import tpu as pltpu
from jax.sharding import PartitionSpec as P

SEQ = 8192
POLES = 16
ROWS = 128
CHANNELS = 512
LANES = 128
SUBS = 8
STEPS = ROWS // SUBS
RING = 8
LINK = jnp.bfloat16

GROUPS = tuple(slice(g * LANES, (g + 1) * LANES) for g in range(CHANNELS // LANES))
Z_GROUPS = [[y * RING + z for z in range(RING)] for y in range(RING)]
Y_GROUPS = [[y * RING + z for y in range(RING)] for z in range(RING)]
TENSOR = 8
DOWN = [(t, (t - 1) % TENSOR) for t in range(TENSOR)]
UP = [(t, (t + 1) % TENSOR) for t in range(TENSOR)]
DOWN_BLOCKS = (-4, -3, -2, -1)
UP_BLOCKS = (3, 2, 1)
LATER_BLOCKS = (-3, 2, -2, 1, -1, 0)


def over_subs(rows):
    return jnp.broadcast_to(rows[:, None, :], (POLES, SUBS, LANES))


def sub_index():
    return lax.broadcasted_iota(jnp.int32, (POLES, SUBS, LANES), 1).astype(jnp.float32)


def end_states(
    gate_hbm, value_hbm, rate_hbm, x_ref, ends_ref, send_ref, gate_ref, value_ref, rate_ref, sems
):
    pairs = ((gate_hbm, gate_ref), (value_hbm, value_ref), (rate_hbm, rate_ref))
    copies = [pltpu.make_async_copy(a, b, sems.at[i]) for i, (a, b) in enumerate(pairs)]
    for copy in copies:
        copy.start()
    for copy in copies:
        copy.wait()
    product = gate_ref[...].astype(jnp.float32) * value_ref[...].astype(jnp.float32)
    product = product.astype(jnp.bfloat16).astype(jnp.float32)
    for g, lanes in enumerate(GROUPS):
        x_ref[g] = product[:, lanes]
        rate = rate_ref[:, lanes] / SEQ
        shrink = over_subs(jnp.exp(-rate))
        state = jnp.zeros((POLES, SUBS, LANES), jnp.float32)
        for t in range(STEPS):
            row = x_ref[g, pl.ds(t, SUBS, stride=STEPS), :]
            state = shrink * state + row[None]
        ends_ref[:, :, lanes] = state
        left = STEPS * (SUBS - 1.0 - sub_index())
        total = jnp.sum(state * jnp.exp(-over_subs(rate) * left), axis=1).astype(LINK)
        for j in range(RING):
            send_ref[j, :, lanes] = total


def chunk_carry(came_ref, rate_ref, prior_ref, send_ref):
    z = lax.rem(lax.axis_index("context"), RING)
    shrink = jnp.exp(-rate_ref[...] * (ROWS / SEQ))
    prior = jnp.zeros((POLES, CHANNELS), jnp.float32)
    total = jnp.zeros((POLES, CHANNELS), jnp.float32)
    for j in range(RING):
        came = came_ref[j].astype(jnp.float32)
        prior = jnp.where(j < z, prior * shrink + came, prior)
        total = total * shrink + came
    prior_ref[...] = prior
    sent = total.astype(LINK)
    for j in range(RING):
        send_ref[j] = sent


def convolve_project(
    came_ref, prior_ref, ends_ref, x_ref, query_ref, residue_ref, rate_ref, weight_ref,
    down_ref, up_ref, gated_ref, y_ref,
):
    context = lax.axis_index("context")
    z, y = lax.rem(context, RING), context // RING
    shrink = jnp.exp(-rate_ref[...] * (RING * ROWS / SEQ))
    carry = jnp.zeros((POLES, CHANNELS), jnp.float32)
    for j in range(RING):
        carry = jnp.where(j < y, carry * shrink + came_ref[j].astype(jnp.float32), carry)
    behind = (z * ROWS).astype(jnp.float32) / SEQ
    carry = carry * jnp.exp(-rate_ref[...] * behind) + prior_ref[...]
    for g, lanes in enumerate(GROUPS):
        rate = rate_ref[:, lanes] / SEQ
        steps = over_subs(rate)
        shrink_sub = jnp.exp(-steps * STEPS)
        sub = sub_index()
        state = jnp.where(sub > 0, pltpu.roll(ends_ref[:, :, lanes], 1, 1), over_subs(carry[:, lanes]))
        for shift in (1, 2, 4):
            state = state + jnp.where(sub >= shift, pltpu.roll(state, shift, 1), 0.0) * shrink_sub
            shrink_sub = shrink_sub * shrink_sub
        shrink_one = over_subs(jnp.exp(-rate))
        residue = over_subs(residue_ref[:, lanes])
        for t in range(STEPS):
            row = x_ref[g, pl.ds(t, SUBS, stride=STEPS), :]
            state = shrink_one * state + row[None]
            y_ref[g, pl.ds(t, SUBS, stride=STEPS), :] = jnp.sum(residue * state, axis=0)
    convolved = jnp.concatenate([y_ref[g] for g in range(len(GROUPS))], axis=1)
    gated = (query_ref[...].astype(jnp.float32) * convolved).astype(jnp.bfloat16)
    gated_ref[...] = gated
    down_ref[...] = project(gated, weight_ref, DOWN_BLOCKS[0]).astype(LINK)
    up_ref[...] = project(gated, weight_ref, UP_BLOCKS[0]).astype(LINK)


def project(gated, weight_ref, offset):
    owner = lax.rem(lax.axis_index("tensor") + (offset + TENSOR), TENSOR)
    column = pl.multiple_of(owner * CHANNELS, CHANNELS)
    return jnp.dot(
        gated, weight_ref[:, pl.ds(column, CHANNELS)], preferred_element_type=jnp.float32
    )


def project_later(gated_ref, weight_ref, *out_refs):
    gated = gated_ref[...]
    for offset, out_ref in zip(LATER_BLOCKS, out_refs):
        out_ref[...] = project(gated, weight_ref, offset)


def add_own(came_ref, own_ref, out_ref):
    out_ref[...] = (came_ref[...].astype(jnp.float32) + own_ref[...]).astype(out_ref.dtype)


def add_both(down_ref, up_ref, own_ref, out_ref):
    total = down_ref[...].astype(jnp.float32) + up_ref[...].astype(jnp.float32) + own_ref[...]
    out_ref[...] = total.astype(out_ref.dtype)


def kernel(body, outs, scratch=(), flops=0, moved=0, **specs):
    return pl.pallas_call(
        body,
        **specs,
        out_shape=[jax.ShapeDtypeStruct(shape, dtype) for shape, dtype in outs],
        scratch_shapes=scratch,
        compiler_params=pltpu.CompilerParams(vmem_limit_bytes=32 * 2**20),
        cost_estimate=pl.CostEstimate(flops=flops, bytes_accessed=moved, transcendentals=0),
    )


def on_device(queries, key_gate, values, residues, decay_rates, out_weight):
    f32, bf16 = jnp.float32, jnp.bfloat16
    block = (RING, POLES, CHANNELS)
    rows, modes = (ROWS, CHANNELS), (POLES, CHANNELS)
    x, ends, sent = kernel(
        end_states,
        [((len(GROUPS), ROWS, LANES), f32), ((POLES, SUBS, CHANNELS), f32), (block, LINK)],
        scratch=[
            pltpu.VMEM(rows, bf16),
            pltpu.VMEM(rows, bf16),
            pltpu.VMEM(modes, f32),
            pltpu.SemaphoreType.DMA((3,)),
        ],
        in_specs=[pl.BlockSpec(memory_space=pltpu.HBM)] * 3,
        flops=8_000_000_000, moved=1_000_000,
    )(*(pltpu.with_memory_space_constraint(a, pltpu.HBM) for a in (key_gate, values, decay_rates)))
    came = lax.all_to_all(sent, "context", 0, 0, axis_index_groups=Z_GROUPS)
    prior, sent = kernel(
        chunk_carry, [(modes, f32), (block, LINK)], flops=8_000_000_000, moved=300_000
    )(came, decay_rates)
    came = lax.all_to_all(sent, "context", 0, 0, axis_index_groups=Y_GROUPS)
    down, up, gated = kernel(
        convolve_project,
        [(rows, LINK), (rows, LINK), (rows, bf16)],
        scratch=[pltpu.VMEM((len(GROUPS), ROWS, LANES), f32)],
        flops=300_000_000, moved=3_000_000,
    )(came, prior, ends, x, queries, residues, decay_rates, out_weight)
    down = lax.ppermute(down, "tensor", DOWN)
    up = lax.ppermute(up, "tensor", UP)
    own = kernel(
        project_later, [(rows, f32)] * len(LATER_BLOCKS), flops=400_000_000, moved=3_000_000
    )(gated, out_weight)
    own = dict(zip(LATER_BLOCKS, own))
    add = kernel(add_own, [(rows, LINK)], flops=100_000, moved=500_000)
    for block in DOWN_BLOCKS[1:]:
        down = lax.ppermute(add(down, own[block])[0], "tensor", DOWN)
    for block in UP_BLOCKS[1:]:
        up = lax.ppermute(add(up, own[block])[0], "tensor", UP)
    (mixed,) = kernel(add_both, [(rows, bf16)], flops=200_000, moved=600_000)(down, up, own[0])
    return mixed


def solution(mesh):
    in_specs = (
        P("context", "tensor"),
        P("context", "tensor"),
        P("context", "tensor"),
        P(None, "tensor"),
        P(None, "tensor"),
        P("tensor", None),
    )
    out_specs = P("context", "tensor")
    return jax.shard_map(
        on_device, mesh=mesh, in_specs=in_specs, out_specs=out_specs, check_vma=False
    )
```

```python
import jax
import jax.numpy as jnp
from jax import lax
from jax.experimental import pallas as pl
from jax.experimental.pallas import tpu as pltpu
from jax.sharding import PartitionSpec as P

SEQ = 8192
POLES = 16
ROWS = 128
CHANNELS = 512
LANES = 128
SUBS = 8
STEPS = ROWS // SUBS
RING = 8
XCHIPS = 4
LINK = jnp.bfloat16

GROUPS = tuple(slice(g * LANES, (g + 1) * LANES) for g in range(CHANNELS // LANES))
Z_GROUPS = [[y * RING + z for z in range(RING)] for y in range(RING)]
Y_GROUPS = [[y * RING + z for y in range(RING)] for z in range(RING)]
X_GROUPS = [[x * 2 + core for x in range(XCHIPS)] for core in range(2)]
SIBLING = [(t, t ^ 1) for t in range(2 * XCHIPS)]


def over_subs(rows):
    return jnp.broadcast_to(rows[:, None, :], (POLES, SUBS, LANES))


def sub_index():
    return lax.broadcasted_iota(jnp.int32, (POLES, SUBS, LANES), 1).astype(jnp.float32)


def end_states(
    gate_hbm, value_hbm, rate_hbm, x_ref, ends_ref, send_ref, gate_ref, value_ref, rate_ref, sems
):
    pairs = ((gate_hbm, gate_ref), (value_hbm, value_ref), (rate_hbm, rate_ref))
    copies = [pltpu.make_async_copy(a, b, sems.at[i]) for i, (a, b) in enumerate(pairs)]
    for copy in copies:
        copy.start()
    for copy in copies:
        copy.wait()
    product = gate_ref[...].astype(jnp.float32) * value_ref[...].astype(jnp.float32)
    product = product.astype(jnp.bfloat16).astype(jnp.float32)
    for g, lanes in enumerate(GROUPS):
        x_ref[g] = product[:, lanes]
        rate = rate_ref[:, lanes] / SEQ
        shrink = over_subs(jnp.exp(-rate))
        state = jnp.zeros((POLES, SUBS, LANES), jnp.float32)
        for t in range(STEPS):
            row = x_ref[g, pl.ds(t, SUBS, stride=STEPS), :]
            state = shrink * state + row[None]
        ends_ref[:, :, lanes] = state
        left = STEPS * (SUBS - 1.0 - sub_index())
        total = jnp.sum(state * jnp.exp(-over_subs(rate) * left), axis=1).astype(LINK)
        for j in range(RING):
            send_ref[j, :, lanes] = total


def row_carry(came_ref, rate_ref, send_ref):
    context = lax.axis_index("context")
    z, y = lax.rem(context, RING), context // RING
    shrink = jnp.exp(-rate_ref[...] * (RING * ROWS / SEQ))
    prior = jnp.zeros((POLES, CHANNELS), jnp.float32)
    for j in range(RING):
        prior = jnp.where(j < y, prior * shrink + came_ref[j].astype(jnp.float32), prior)
    alone = prior.astype(LINK)
    both = (prior * shrink + came_ref[y].astype(jnp.float32)).astype(LINK)
    for j in range(RING):
        send_ref[j] = jnp.where(j > z, both, alone)


def convolve_project(
    came_ref, ends_ref, x_ref, query_ref, residue_ref, rate_ref, weight_ref,
    send_ref, gated_ref, y_ref,
):
    core = lax.rem(lax.axis_index("tensor"), 2)
    z = lax.rem(lax.axis_index("context"), RING)
    shrink = jnp.exp(-rate_ref[...] * (ROWS / SEQ))
    carry = jnp.zeros((POLES, CHANNELS), jnp.float32)
    for j in range(RING):
        carry = carry * shrink + came_ref[lax.rem(z + j, RING)].astype(jnp.float32)
    for g, lanes in enumerate(GROUPS):
        rate = rate_ref[:, lanes] / SEQ
        steps = over_subs(rate)
        shrink_sub = jnp.exp(-steps * STEPS)
        sub = sub_index()
        state = jnp.where(sub > 0, pltpu.roll(ends_ref[:, :, lanes], 1, 1), over_subs(carry[:, lanes]))
        for shift in (1, 2, 4):
            state = state + jnp.where(sub >= shift, pltpu.roll(state, shift, 1), 0.0) * shrink_sub
            shrink_sub = shrink_sub * shrink_sub
        shrink_one = over_subs(jnp.exp(-rate))
        residue = over_subs(residue_ref[:, lanes])
        for t in range(STEPS):
            row = x_ref[g, pl.ds(t, SUBS, stride=STEPS), :]
            state = shrink_one * state + row[None]
            y_ref[g, pl.ds(t, SUBS, stride=STEPS), :] = jnp.sum(residue * state, axis=0)
    convolved = jnp.concatenate([y_ref[g] for g in range(len(GROUPS))], axis=1)
    gated = (query_ref[...].astype(jnp.float32) * convolved).astype(jnp.bfloat16)
    gated_ref[...] = gated
    project(gated, weight_ref, 1 - core, send_ref)


def project(gated, weight_ref, core, out_ref):
    for chip in range(XCHIPS):
        column = pl.multiple_of((2 * chip + core) * CHANNELS, CHANNELS)
        partial = jnp.dot(
            gated, weight_ref[:, pl.ds(column, CHANNELS)], preferred_element_type=jnp.float32
        )
        out_ref[chip] = partial.astype(out_ref.dtype)


def project_own(gated_ref, weight_ref, keep_ref):
    project(gated_ref[...], weight_ref, lax.rem(lax.axis_index("tensor"), 2), keep_ref)


def add_pair(kept_ref, came_ref, out_ref):
    total = kept_ref[...].astype(jnp.float32) + came_ref[...].astype(jnp.float32)
    out_ref[...] = total.astype(out_ref.dtype)


def add_chips(came_ref, out_ref):
    total = came_ref[0].astype(jnp.float32)
    for chip in range(1, XCHIPS):
        total = total + came_ref[chip].astype(jnp.float32)
    out_ref[...] = total.astype(out_ref.dtype)


def kernel(body, outs, scratch=(), flops=0, moved=0, **specs):
    return pl.pallas_call(
        body,
        **specs,
        out_shape=[jax.ShapeDtypeStruct(shape, dtype) for shape, dtype in outs],
        scratch_shapes=scratch,
        compiler_params=pltpu.CompilerParams(vmem_limit_bytes=32 * 2**20),
        cost_estimate=pl.CostEstimate(flops=flops, bytes_accessed=moved, transcendentals=0),
    )


def on_device(queries, key_gate, values, residues, decay_rates, out_weight):
    f32, bf16 = jnp.float32, jnp.bfloat16
    block = (RING, POLES, CHANNELS)
    rows, modes = (ROWS, CHANNELS), (POLES, CHANNELS)
    x, ends, sent = kernel(
        end_states,
        [((len(GROUPS), ROWS, LANES), f32), ((POLES, SUBS, CHANNELS), f32), (block, LINK)],
        scratch=[
            pltpu.VMEM(rows, bf16),
            pltpu.VMEM(rows, bf16),
            pltpu.VMEM(modes, f32),
            pltpu.SemaphoreType.DMA((3,)),
        ],
        in_specs=[pl.BlockSpec(memory_space=pltpu.HBM)] * 3,
        flops=8_000_000_000, moved=1_000_000,
    )(*(pltpu.with_memory_space_constraint(a, pltpu.HBM) for a in (key_gate, values, decay_rates)))
    came = lax.all_to_all(sent, "context", 0, 0, axis_index_groups=Y_GROUPS)
    (sent,) = kernel(row_carry, [(block, LINK)], flops=8_000_000_000, moved=300_000)(
        came, decay_rates
    )
    came = lax.all_to_all(sent, "context", 0, 0, axis_index_groups=Z_GROUPS)
    halves = (XCHIPS, ROWS, CHANNELS)
    sent, gated = kernel(
        convolve_project,
        [(halves, bf16), (rows, bf16)],
        scratch=[pltpu.VMEM((len(GROUPS), ROWS, LANES), f32)],
        flops=300_000_000, moved=3_000_000,
    )(came, ends, x, queries, residues, decay_rates, out_weight)
    came = lax.ppermute(sent, "tensor", SIBLING)
    (kept,) = kernel(project_own, [(halves, f32)], flops=600_000_000, moved=3_000_000)(
        gated, out_weight
    )
    (pair,) = kernel(add_pair, [(halves, bf16)], flops=300_000, moved=1_500_000)(kept, came)
    came = lax.all_to_all(pair, "tensor", 0, 0, axis_index_groups=X_GROUPS)
    (mixed,) = kernel(add_chips, [(rows, bf16)], flops=300_000, moved=700_000)(came)
    return mixed


def solution(mesh):
    in_specs = (
        P("context", "tensor"),
        P("context", "tensor"),
        P("context", "tensor"),
        P(None, "tensor"),
        P(None, "tensor"),
        P("tensor", None),
    )
    out_specs = P("context", "tensor")
    return jax.shard_map(
        on_device, mesh=mesh, in_specs=in_specs, out_specs=out_specs, check_vma=False
    )
```

```python
import jax
import jax.numpy as jnp
from jax import lax
from jax.experimental import pallas as pl
from jax.experimental.pallas import tpu as pltpu
from jax.sharding import PartitionSpec as P

SEQ = 8192
POLES = 16
ROWS = 128
CHANNELS = 512
LANES = 128
SUBS = 8
STEPS = ROWS // SUBS
RING = 8
XCHIPS = 4
LINK = jnp.bfloat16

GROUPS = tuple(slice(g * LANES, (g + 1) * LANES) for g in range(CHANNELS // LANES))
Z_GROUPS = [[y * RING + z for z in range(RING)] for y in range(RING)]
Y_GROUPS = [[y * RING + z for y in range(RING)] for z in range(RING)]
X_GROUPS = [[x * 2 + core for x in range(XCHIPS)] for core in range(2)]
CORE_GROUPS = [[2 * x, 2 * x + 1] for x in range(XCHIPS)]


def over_subs(rows):
    return jnp.broadcast_to(rows[:, None, :], (POLES, SUBS, LANES))


def sub_index():
    return lax.broadcasted_iota(jnp.int32, (POLES, SUBS, LANES), 1).astype(jnp.float32)


def weight_copies(weight_hbm, weight_ref, sems):
    core = lax.rem(lax.axis_index("tensor"), 2)
    copies = []
    for chip in range(XCHIPS):
        columns = pl.ds(pl.multiple_of((2 * chip + core) * CHANNELS, CHANNELS), CHANNELS)
        copies.append(
            pltpu.make_async_copy(weight_hbm.at[:, columns], weight_ref.at[chip], sems.at[chip])
        )
    return copies


def end_states(
    gate_hbm, value_hbm, rate_hbm, weight_hbm, x_ref, ends_ref, send_ref, weight_ref,
    gate_ref, value_ref, rate_ref, sems, weight_sems,
):
    pairs = ((gate_hbm, gate_ref), (value_hbm, value_ref), (rate_hbm, rate_ref))
    copies = [pltpu.make_async_copy(a, b, sems.at[i]) for i, (a, b) in enumerate(pairs)]
    later = weight_copies(weight_hbm, weight_ref, weight_sems)
    for copy in copies + later:
        copy.start()
    for copy in copies:
        copy.wait()
    product = gate_ref[...].astype(jnp.float32) * value_ref[...].astype(jnp.float32)
    product = product.astype(jnp.bfloat16).astype(jnp.float32)
    for g, lanes in enumerate(GROUPS):
        x_ref[g] = product[:, lanes]
        rate = rate_ref[:, lanes] / SEQ
        shrink = over_subs(jnp.exp(-rate))
        state = jnp.zeros((POLES, SUBS, LANES), jnp.float32)
        for t in range(STEPS):
            row = x_ref[g, pl.ds(t, SUBS, stride=STEPS), :]
            state = shrink * state + row[None]
        ends_ref[:, :, lanes] = state
        left = STEPS * (SUBS - 1.0 - sub_index())
        total = jnp.sum(state * jnp.exp(-over_subs(rate) * left), axis=1).astype(LINK)
        for j in range(RING):
            send_ref[j, :, lanes] = total
    for copy in later:
        copy.wait()


def row_carry(came_ref, rate_ref, send_ref):
    context = lax.axis_index("context")
    z, y = lax.rem(context, RING), context // RING
    shrink = jnp.exp(-rate_ref[...] * (RING * ROWS / SEQ))
    prior = jnp.zeros((POLES, CHANNELS), jnp.float32)
    for j in range(RING):
        prior = jnp.where(j < y, prior * shrink + came_ref[j].astype(jnp.float32), prior)
    alone = prior.astype(LINK)
    both = (prior * shrink + came_ref[y].astype(jnp.float32)).astype(LINK)
    for j in range(RING):
        send_ref[j] = jnp.where(j > z, both, alone)


def convolve_gate(
    came_ref, ends_ref, x_ref, query_ref, residue_ref, rate_ref, weights_hbm,
    gated_ref, weight_ref, y_ref, sems,
):
    core = lax.rem(lax.axis_index("tensor"), 2)
    copies = weight_copies(weights_hbm.at[1 - core], weight_ref, sems)
    for copy in copies:
        copy.start()
    z = lax.rem(lax.axis_index("context"), RING)
    shrink = jnp.exp(-rate_ref[...] * (ROWS / SEQ))
    carry = jnp.zeros((POLES, CHANNELS), jnp.float32)
    for j in range(RING):
        carry = carry * shrink + came_ref[lax.rem(z + j, RING)].astype(jnp.float32)
    for g, lanes in enumerate(GROUPS):
        rate = rate_ref[:, lanes] / SEQ
        steps = over_subs(rate)
        shrink_sub = jnp.exp(-steps * STEPS)
        sub = sub_index()
        state = jnp.where(sub > 0, pltpu.roll(ends_ref[:, :, lanes], 1, 1), over_subs(carry[:, lanes]))
        for shift in (1, 2, 4):
            state = state + jnp.where(sub >= shift, pltpu.roll(state, shift, 1), 0.0) * shrink_sub
            shrink_sub = shrink_sub * shrink_sub
        shrink_one = over_subs(jnp.exp(-rate))
        residue = over_subs(residue_ref[:, lanes])
        for t in range(STEPS):
            row = x_ref[g, pl.ds(t, SUBS, stride=STEPS), :]
            state = shrink_one * state + row[None]
            y_ref[g, pl.ds(t, SUBS, stride=STEPS), :] = jnp.sum(residue * state, axis=0)
    convolved = jnp.concatenate([y_ref[g] for g in range(len(GROUPS))], axis=1)
    gated = query_ref[...].astype(jnp.float32) * convolved
    gated_ref[...] = gated.astype(jnp.bfloat16)
    for copy in copies:
        copy.wait()


def project(gated_ref, weight_ref, sibling_ref, out_ref):
    core = lax.rem(lax.axis_index("tensor"), 2)
    mine, other = gated_ref[core], gated_ref[1 - core]
    for chip in range(XCHIPS):
        partial = jnp.dot(
            mine, weight_ref[chip], preferred_element_type=jnp.float32
        ) + jnp.dot(other, sibling_ref[chip], preferred_element_type=jnp.float32)
        out_ref[chip] = partial.astype(out_ref.dtype)


def add_chips(came_ref, out_ref):
    total = came_ref[0].astype(jnp.float32)
    for chip in range(1, XCHIPS):
        total = total + came_ref[chip].astype(jnp.float32)
    out_ref[...] = total.astype(out_ref.dtype)


def kernel(body, outs, scratch=(), flops=0, moved=0, **specs):
    return pl.pallas_call(
        body,
        **specs,
        out_shape=[jax.ShapeDtypeStruct(shape, dtype) for shape, dtype in outs],
        scratch_shapes=scratch,
        compiler_params=pltpu.CompilerParams(vmem_limit_bytes=32 * 2**20),
        cost_estimate=pl.CostEstimate(flops=flops, bytes_accessed=moved, transcendentals=0),
    )


def in_hbm(array):
    return pltpu.with_memory_space_constraint(array, pltpu.HBM)


def on_device(queries, key_gate, values, residues, decay_rates, out_weight):
    f32, bf16 = jnp.float32, jnp.bfloat16
    block = (RING, POLES, CHANNELS)
    rows, modes = (ROWS, CHANNELS), (POLES, CHANNELS)
    columns = (XCHIPS, CHANNELS, CHANNELS)
    weights = lax.all_gather(out_weight, "tensor", axis_index_groups=CORE_GROUPS)
    x, ends, sent, own = kernel(
        end_states,
        [
            ((len(GROUPS), ROWS, LANES), f32),
            ((POLES, SUBS, CHANNELS), f32),
            (block, LINK),
            (columns, bf16),
        ],
        scratch=[
            pltpu.VMEM(rows, bf16),
            pltpu.VMEM(rows, bf16),
            pltpu.VMEM(modes, f32),
            pltpu.SemaphoreType.DMA((3,)),
            pltpu.SemaphoreType.DMA((XCHIPS,)),
        ],
        in_specs=[pl.BlockSpec(memory_space=pltpu.HBM)] * 4,
        flops=8_000_000_000, moved=1_000_000,
    )(*map(in_hbm, (key_gate, values, decay_rates, out_weight)))
    came = lax.all_to_all(sent, "context", 0, 0, axis_index_groups=Y_GROUPS)
    (sent,) = kernel(row_carry, [(block, LINK)], flops=8_000_000_000, moved=300_000)(
        came, decay_rates
    )
    came = lax.all_to_all(sent, "context", 0, 0, axis_index_groups=Z_GROUPS)
    halves = (XCHIPS, ROWS, CHANNELS)
    gated, sibling = kernel(
        convolve_gate,
        [(rows, bf16), (columns, bf16)],
        scratch=[
            pltpu.VMEM((len(GROUPS), ROWS, LANES), f32),
            pltpu.SemaphoreType.DMA((XCHIPS,)),
        ],
        in_specs=[pl.BlockSpec(memory_space=pltpu.VMEM)] * 6
        + [pl.BlockSpec(memory_space=pltpu.HBM)],
        flops=100_000, moved=10_000,
    )(
        came, ends, x, queries, residues, decay_rates,
        in_hbm(weights),
    )
    both = lax.all_gather(gated, "tensor", axis_index_groups=CORE_GROUPS)
    (pair,) = kernel(project, [(halves, bf16)], flops=600_000_000, moved=5_000_000)(
        both, own, sibling
    )
    came = lax.all_to_all(pair, "tensor", 0, 0, axis_index_groups=X_GROUPS)
    (mixed,) = kernel(add_chips, [(rows, bf16)], flops=300_000, moved=700_000)(came)
    return mixed


def solution(mesh):
    in_specs = (
        P("context", "tensor"),
        P("context", "tensor"),
        P("context", "tensor"),
        P(None, "tensor"),
        P(None, "tensor"),
        P("tensor", None),
    )
    out_specs = P("context", "tensor")
    return jax.shard_map(
        on_device, mesh=mesh, in_specs=in_specs, out_specs=out_specs, check_vma=False
    )
```

```python
import jax
import jax.numpy as jnp
from jax import lax
from jax.experimental import pallas as pl
from jax.experimental.pallas import tpu as pltpu
from jax.sharding import PartitionSpec as P

SEQ = 8192
POLES = 16
ROWS = 128
CHANNELS = 512
LANES = 128
SUBS = 8
STEPS = ROWS // SUBS
RING = 8
XCHIPS = 4
LINK = jnp.bfloat16

GROUPS = tuple(slice(g * LANES, (g + 1) * LANES) for g in range(CHANNELS // LANES))
Z_GROUPS = [[y * RING + z for z in range(RING)] for y in range(RING)]
Y_GROUPS = [[y * RING + z for y in range(RING)] for z in range(RING)]
X_GROUPS = [[x * 2 + core for x in range(XCHIPS)] for core in range(2)]
CORE_GROUPS = [[2 * x, 2 * x + 1] for x in range(XCHIPS)]
TENSOR = 2 * XCHIPS
UP = [(t, (t + 1) % TENSOR) for t in range(TENSOR)]
DOWN = [(t, (t - 1) % TENSOR) for t in range(TENSOR)]


def over_subs(rows):
    return jnp.broadcast_to(rows[:, None, :], (POLES, SUBS, LANES))


def sub_index():
    return lax.broadcasted_iota(jnp.int32, (POLES, SUBS, LANES), 1).astype(jnp.float32)


def end_states(
    gate_hbm, value_hbm, rate_hbm, x_ref, ends_ref, send_ref, gate_ref, value_ref, rate_ref, sems
):
    pairs = ((gate_hbm, gate_ref), (value_hbm, value_ref), (rate_hbm, rate_ref))
    copies = [pltpu.make_async_copy(a, b, sems.at[i]) for i, (a, b) in enumerate(pairs)]
    for copy in copies:
        copy.start()
    for copy in copies:
        copy.wait()
    product = gate_ref[...].astype(jnp.float32) * value_ref[...].astype(jnp.float32)
    product = product.astype(jnp.bfloat16).astype(jnp.float32)
    for g, lanes in enumerate(GROUPS):
        x_ref[g] = product[:, lanes]
        rate = rate_ref[:, lanes] / SEQ
        shrink = over_subs(jnp.exp(-rate))
        state = jnp.zeros((POLES, SUBS, LANES), jnp.float32)
        for t in range(STEPS):
            row = x_ref[g, pl.ds(t, SUBS, stride=STEPS), :]
            state = shrink * state + row[None]
        ends_ref[:, :, lanes] = state
        left = STEPS * (SUBS - 1.0 - sub_index())
        total = jnp.sum(state * jnp.exp(-over_subs(rate) * left), axis=1).astype(LINK)
        for j in range(RING):
            send_ref[j, :, lanes] = total


def row_carry(came_ref, rate_ref, send_ref):
    context = lax.axis_index("context")
    z, y = lax.rem(context, RING), context // RING
    shrink = jnp.exp(-rate_ref[...] * (RING * ROWS / SEQ))
    prior = jnp.zeros((POLES, CHANNELS), jnp.float32)
    for j in range(RING):
        prior = jnp.where(j < y, prior * shrink + came_ref[j].astype(jnp.float32), prior)
    alone = prior.astype(LINK)
    both = (prior * shrink + came_ref[y].astype(jnp.float32)).astype(LINK)
    for j in range(RING):
        send_ref[j] = jnp.where(j > z, both, alone)


def convolve_gate(
    came_ref, ends_ref, x_ref, query_ref, residue_ref, rate_ref, gated_ref, y_ref,
):
    z = lax.rem(lax.axis_index("context"), RING)
    shrink = jnp.exp(-rate_ref[...] * (ROWS / SEQ))
    carry = jnp.zeros((POLES, CHANNELS), jnp.float32)
    for j in range(RING):
        carry = carry * shrink + came_ref[lax.rem(z + j, RING)].astype(jnp.float32)
    for g, lanes in enumerate(GROUPS):
        rate = rate_ref[:, lanes] / SEQ
        steps = over_subs(rate)
        shrink_sub = jnp.exp(-steps * STEPS)
        sub = sub_index()
        state = jnp.where(sub > 0, pltpu.roll(ends_ref[:, :, lanes], 1, 1), over_subs(carry[:, lanes]))
        for shift in (1, 2, 4):
            state = state + jnp.where(sub >= shift, pltpu.roll(state, shift, 1), 0.0) * shrink_sub
            shrink_sub = shrink_sub * shrink_sub
        shrink_one = over_subs(jnp.exp(-rate))
        residue = over_subs(residue_ref[:, lanes])
        for t in range(STEPS):
            row = x_ref[g, pl.ds(t, SUBS, stride=STEPS), :]
            state = shrink_one * state + row[None]
            y_ref[g, pl.ds(t, SUBS, stride=STEPS), :] = jnp.sum(residue * state, axis=0)
    convolved = jnp.concatenate([y_ref[g] for g in range(len(GROUPS))], axis=1)
    gated = query_ref[...].astype(jnp.float32) * convolved
    gated_ref[...] = gated.astype(jnp.bfloat16)


def project(gated_ref, weight_ref, up_ref, down_ref, out_ref):
    for core, sibling_ref in ((0, down_ref), (1, up_ref)):

        @pl.when(lax.rem(lax.axis_index("tensor"), 2) == core)
        def _():
            for chip in range(XCHIPS):
                columns = pl.ds((2 * chip + core) * CHANNELS, CHANNELS)
                partial = jnp.dot(
                    gated_ref[core], weight_ref[:, columns], preferred_element_type=jnp.float32
                ) + jnp.dot(
                    gated_ref[1 - core], sibling_ref[:, columns], preferred_element_type=jnp.float32
                )
                out_ref[chip] = partial.astype(out_ref.dtype)


def add_chips(came_ref, out_ref):
    total = came_ref[0].astype(jnp.float32)
    for chip in range(1, XCHIPS):
        total = total + came_ref[chip].astype(jnp.float32)
    out_ref[...] = total.astype(out_ref.dtype)


def kernel(body, outs, scratch=(), flops=0, moved=0, **specs):
    return pl.pallas_call(
        body,
        **specs,
        out_shape=[jax.ShapeDtypeStruct(shape, dtype) for shape, dtype in outs],
        scratch_shapes=scratch,
        compiler_params=pltpu.CompilerParams(vmem_limit_bytes=32 * 2**20),
        cost_estimate=pl.CostEstimate(flops=flops, bytes_accessed=moved, transcendentals=0),
    )


def on_device(queries, key_gate, values, residues, decay_rates, out_weight):
    f32, bf16 = jnp.float32, jnp.bfloat16
    block = (RING, POLES, CHANNELS)
    up = lax.ppermute(out_weight, "tensor", UP)
    down = lax.ppermute(out_weight, "tensor", DOWN)
    rows, modes = (ROWS, CHANNELS), (POLES, CHANNELS)
    x, ends, sent = kernel(
        end_states,
        [((len(GROUPS), ROWS, LANES), f32), ((POLES, SUBS, CHANNELS), f32), (block, LINK)],
        scratch=[
            pltpu.VMEM(rows, bf16),
            pltpu.VMEM(rows, bf16),
            pltpu.VMEM(modes, f32),
            pltpu.SemaphoreType.DMA((3,)),
        ],
        in_specs=[pl.BlockSpec(memory_space=pltpu.HBM)] * 3,
        flops=8_000_000_000, moved=1_000_000,
    )(*(pltpu.with_memory_space_constraint(a, pltpu.HBM) for a in (key_gate, values, decay_rates)))
    came = lax.all_to_all(sent, "context", 0, 0, axis_index_groups=Y_GROUPS)
    (sent,) = kernel(row_carry, [(block, LINK)], flops=8_000_000_000, moved=300_000)(
        came, decay_rates
    )
    came = lax.all_to_all(sent, "context", 0, 0, axis_index_groups=Z_GROUPS)
    halves = (XCHIPS, ROWS, CHANNELS)
    (gated,) = kernel(
        convolve_gate,
        [(rows, bf16)],
        scratch=[pltpu.VMEM((len(GROUPS), ROWS, LANES), f32)],
        flops=100_000, moved=10_000,
    )(came, ends, x, queries, residues, decay_rates)
    both = lax.all_gather(gated, "tensor", axis_index_groups=CORE_GROUPS)
    (pair,) = kernel(project, [(halves, bf16)], flops=600_000_000, moved=5_000_000)(
        both, out_weight, up, down
    )
    came = lax.all_to_all(pair, "tensor", 0, 0, axis_index_groups=X_GROUPS)
    (mixed,) = kernel(add_chips, [(rows, bf16)], flops=300_000, moved=700_000)(came)
    return mixed


def solution(mesh):
    in_specs = (
        P("context", "tensor"),
        P("context", "tensor"),
        P("context", "tensor"),
        P(None, "tensor"),
        P(None, "tensor"),
        P("tensor", None),
    )
    out_specs = P("context", "tensor")
    return jax.shard_map(
        on_device, mesh=mesh, in_specs=in_specs, out_specs=out_specs, check_vma=False
    )
```

```python
import jax
import jax.numpy as jnp
from jax import lax
from jax.experimental import pallas as pl
from jax.experimental.pallas import tpu as pltpu
from jax.sharding import PartitionSpec as P

SEQ = 8192
POLES = 16
ROWS = 128
CHANNELS = 512
LANES = 128
SUBS = 8
STEPS = ROWS // SUBS
RING = 8
XCHIPS = 4
LINK = jnp.bfloat16

GROUPS = tuple(slice(g * LANES, (g + 1) * LANES) for g in range(CHANNELS // LANES))
ORDER = (0, 4, 2, 6, 1, 5, 3, 7)
X_ORDER = (0, 2, 1, 3)
Z_GROUPS = [[y * RING + z for z in ORDER] for y in range(RING)]
Y_GROUPS = [[y * RING + z for y in ORDER] for z in range(RING)]
X_GROUPS = [[x * 2 + core for x in X_ORDER] for core in range(2)]
SIBLING = [(t, t ^ 1) for t in range(2 * XCHIPS)]


def over_subs(rows):
    return jnp.broadcast_to(rows[:, None, :], (POLES, SUBS, LANES))


def sub_index():
    return lax.broadcasted_iota(jnp.int32, (POLES, SUBS, LANES), 1).astype(jnp.float32)


def end_states(
    gate_hbm, value_hbm, rate_hbm, x_ref, ends_ref, send_ref, gate_ref, value_ref, rate_ref, sems
):
    pairs = ((gate_hbm, gate_ref), (value_hbm, value_ref), (rate_hbm, rate_ref))
    copies = [pltpu.make_async_copy(a, b, sems.at[i]) for i, (a, b) in enumerate(pairs)]
    for copy in copies:
        copy.start()
    for copy in copies:
        copy.wait()
    product = gate_ref[...].astype(jnp.float32) * value_ref[...].astype(jnp.float32)
    product = product.astype(jnp.bfloat16).astype(jnp.float32)
    for g, lanes in enumerate(GROUPS):
        x_ref[g] = product[:, lanes]
        rate = rate_ref[:, lanes] / SEQ
        shrink = over_subs(jnp.exp(-rate))
        state = jnp.zeros((POLES, SUBS, LANES), jnp.float32)
        for t in range(STEPS):
            row = x_ref[g, pl.ds(t, SUBS, stride=STEPS), :]
            state = shrink * state + row[None]
        ends_ref[:, :, lanes] = state
        left = STEPS * (SUBS - 1.0 - sub_index())
        total = jnp.sum(state * jnp.exp(-over_subs(rate) * left), axis=1).astype(LINK)
        for j in range(RING):
            send_ref[j, :, lanes] = total


def place_of(chip):
    return 4 * lax.rem(chip, 2) + 2 * lax.rem(chip // 2, 2) + chip // 4


def row_carry(came_ref, rate_ref, send_ref):
    context = lax.axis_index("context")
    z, y = lax.rem(context, RING), context // RING
    shrink = jnp.exp(-rate_ref[...] * (RING * ROWS / SEQ))
    prior = jnp.zeros((POLES, CHANNELS), jnp.float32)
    for j in range(RING):
        came = came_ref[ORDER[j]].astype(jnp.float32)
        prior = jnp.where(j < y, prior * shrink + came, prior)
    alone = prior.astype(LINK)
    both = (prior * shrink + came_ref[place_of(y)].astype(jnp.float32)).astype(LINK)
    for j in range(RING):
        send_ref[ORDER[j]] = jnp.where(j > z, both, alone)


def convolve_project(
    came_ref, ends_ref, x_ref, query_ref, residue_ref, rate_ref, weight_ref,
    send_ref, gated_ref, y_ref,
):
    core = lax.rem(lax.axis_index("tensor"), 2)
    z = lax.rem(lax.axis_index("context"), RING)
    shrink = jnp.exp(-rate_ref[...] * (ROWS / SEQ))
    carry = jnp.zeros((POLES, CHANNELS), jnp.float32)
    for j in range(RING):
        came = came_ref[place_of(lax.rem(z + j, RING))].astype(jnp.float32)
        carry = carry * shrink + came
    for g, lanes in enumerate(GROUPS):
        rate = rate_ref[:, lanes] / SEQ
        steps = over_subs(rate)
        shrink_sub = jnp.exp(-steps * STEPS)
        sub = sub_index()
        state = jnp.where(sub > 0, pltpu.roll(ends_ref[:, :, lanes], 1, 1), over_subs(carry[:, lanes]))
        for shift in (1, 2, 4):
            state = state + jnp.where(sub >= shift, pltpu.roll(state, shift, 1), 0.0) * shrink_sub
            shrink_sub = shrink_sub * shrink_sub
        shrink_one = over_subs(jnp.exp(-rate))
        residue = over_subs(residue_ref[:, lanes])
        for t in range(STEPS):
            row = x_ref[g, pl.ds(t, SUBS, stride=STEPS), :]
            state = shrink_one * state + row[None]
            y_ref[g, pl.ds(t, SUBS, stride=STEPS), :] = jnp.sum(residue * state, axis=0)
    convolved = jnp.concatenate([y_ref[g] for g in range(len(GROUPS))], axis=1)
    gated = (query_ref[...].astype(jnp.float32) * convolved).astype(jnp.bfloat16)
    gated_ref[...] = gated
    project(gated, weight_ref, 1 - core, send_ref)


def project(gated, weight_ref, core, out_ref):
    for place, chip in enumerate(X_ORDER):
        column = pl.multiple_of((2 * chip + core) * CHANNELS, CHANNELS)
        partial = jnp.dot(
            gated, weight_ref[:, pl.ds(column, CHANNELS)], preferred_element_type=jnp.float32
        )
        out_ref[place] = partial.astype(out_ref.dtype)


def project_own(gated_ref, weight_ref, keep_ref):
    project(gated_ref[...], weight_ref, lax.rem(lax.axis_index("tensor"), 2), keep_ref)


def add_pair(kept_ref, came_ref, out_ref):
    total = kept_ref[...].astype(jnp.float32) + came_ref[...].astype(jnp.float32)
    out_ref[...] = total.astype(out_ref.dtype)


def add_chips(came_ref, out_ref):
    total = came_ref[0].astype(jnp.float32)
    for chip in range(1, XCHIPS):
        total = total + came_ref[chip].astype(jnp.float32)
    out_ref[...] = total.astype(out_ref.dtype)


def kernel(body, outs, scratch=(), flops=0, moved=0, **specs):
    return pl.pallas_call(
        body,
        **specs,
        out_shape=[jax.ShapeDtypeStruct(shape, dtype) for shape, dtype in outs],
        scratch_shapes=scratch,
        compiler_params=pltpu.CompilerParams(vmem_limit_bytes=32 * 2**20),
        cost_estimate=pl.CostEstimate(flops=flops, bytes_accessed=moved, transcendentals=0),
    )


def on_device(queries, key_gate, values, residues, decay_rates, out_weight):
    f32, bf16 = jnp.float32, jnp.bfloat16
    block = (RING, POLES, CHANNELS)
    rows, modes = (ROWS, CHANNELS), (POLES, CHANNELS)
    x, ends, sent = kernel(
        end_states,
        [((len(GROUPS), ROWS, LANES), f32), ((POLES, SUBS, CHANNELS), f32), (block, LINK)],
        scratch=[
            pltpu.VMEM(rows, bf16),
            pltpu.VMEM(rows, bf16),
            pltpu.VMEM(modes, f32),
            pltpu.SemaphoreType.DMA((3,)),
        ],
        in_specs=[pl.BlockSpec(memory_space=pltpu.HBM)] * 3,
        flops=8_000_000_000, moved=1_000_000,
    )(*(pltpu.with_memory_space_constraint(a, pltpu.HBM) for a in (key_gate, values, decay_rates)))
    came = lax.all_to_all(sent, "context", 0, 0, axis_index_groups=Y_GROUPS)
    (sent,) = kernel(row_carry, [(block, LINK)], flops=8_000_000_000, moved=300_000)(
        came, decay_rates
    )
    came = lax.all_to_all(sent, "context", 0, 0, axis_index_groups=Z_GROUPS)
    halves = (XCHIPS, ROWS, CHANNELS)
    sent, gated = kernel(
        convolve_project,
        [(halves, bf16), (rows, bf16)],
        scratch=[pltpu.VMEM((len(GROUPS), ROWS, LANES), f32)],
        flops=300_000_000, moved=3_000_000,
    )(came, ends, x, queries, residues, decay_rates, out_weight)
    came = lax.ppermute(sent, "tensor", SIBLING)
    (kept,) = kernel(project_own, [(halves, f32)], flops=600_000_000, moved=3_000_000)(
        gated, out_weight
    )
    (pair,) = kernel(add_pair, [(halves, bf16)], flops=300_000, moved=1_500_000)(kept, came)
    came = lax.all_to_all(pair, "tensor", 0, 0, axis_index_groups=X_GROUPS)
    (mixed,) = kernel(add_chips, [(rows, bf16)], flops=300_000, moved=700_000)(came)
    return mixed


def solution(mesh):
    in_specs = (
        P("context", "tensor"),
        P("context", "tensor"),
        P("context", "tensor"),
        P(None, "tensor"),
        P(None, "tensor"),
        P("tensor", None),
    )
    out_specs = P("context", "tensor")
    return jax.shard_map(
        on_device, mesh=mesh, in_specs=in_specs, out_specs=out_specs, check_vma=False
    )
```

```python
import jax
import jax.numpy as jnp
from jax import lax
from jax.experimental import pallas as pl
from jax.experimental.pallas import tpu as pltpu
from jax.sharding import PartitionSpec as P

SEQ = 8192
POLES = 16
ROWS = 128
CHANNELS = 512
LANES = 128
SUBS = 8
STEPS = ROWS // SUBS
RING = 8
XCHIPS = 4
LINK = jnp.bfloat16

GROUPS = tuple(slice(g * LANES, (g + 1) * LANES) for g in range(CHANNELS // LANES))
Y_ORDER = (4, 0, 6, 2, 5, 1, 7, 3)
Z_ORDER = (4, 0, 6, 2, 5, 1, 7, 3)
X_ORDER = (3, 1, 2, 0)
Z_GROUPS = [[y * RING + z for z in Z_ORDER] for y in range(RING)]
Y_GROUPS = [[y * RING + z for y in Y_ORDER] for z in range(RING)]
X_GROUPS = [[x * 2 + core for x in X_ORDER] for core in range(2)]
SIBLING = [(t, t ^ 1) for t in range(2 * XCHIPS)]


def over_subs(rows):
    return jnp.broadcast_to(rows[:, None, :], (POLES, SUBS, LANES))


def sub_index():
    return lax.broadcasted_iota(jnp.int32, (POLES, SUBS, LANES), 1).astype(jnp.float32)


def end_states(
    gate_hbm, value_hbm, rate_hbm, x_ref, ends_ref, send_ref, gate_ref, value_ref, rate_ref, sems
):
    pairs = ((gate_hbm, gate_ref), (value_hbm, value_ref), (rate_hbm, rate_ref))
    copies = [pltpu.make_async_copy(a, b, sems.at[i]) for i, (a, b) in enumerate(pairs)]
    for copy in copies:
        copy.start()
    for copy in copies:
        copy.wait()
    product = gate_ref[...].astype(jnp.float32) * value_ref[...].astype(jnp.float32)
    product = product.astype(jnp.bfloat16).astype(jnp.float32)
    for g, lanes in enumerate(GROUPS):
        x_ref[g] = product[:, lanes]
        rate = rate_ref[:, lanes] / SEQ
        shrink = over_subs(jnp.exp(-rate))
        state = jnp.zeros((POLES, SUBS, LANES), jnp.float32)
        for t in range(STEPS):
            row = x_ref[g, pl.ds(t, SUBS, stride=STEPS), :]
            state = shrink * state + row[None]
        ends_ref[:, :, lanes] = state
        left = STEPS * (SUBS - 1.0 - sub_index())
        total = jnp.sum(state * jnp.exp(-over_subs(rate) * left), axis=1).astype(LINK)
        for j in range(RING):
            send_ref[j, :, lanes] = total


def place_of(chip, order):
    place = 0
    for index in range(1, RING):
        place = jnp.where(chip == order[index], index, place)
    return place


def row_carry(came_ref, rate_ref, send_ref):
    context = lax.axis_index("context")
    z, y = lax.rem(context, RING), context // RING
    shrink = jnp.exp(-rate_ref[...] * (RING * ROWS / SEQ))
    prior = jnp.zeros((POLES, CHANNELS), jnp.float32)
    for j in range(RING):
        came = came_ref[Y_ORDER.index(j)].astype(jnp.float32)
        prior = jnp.where(j < y, prior * shrink + came, prior)
    alone = prior.astype(LINK)
    both = (prior * shrink + came_ref[place_of(y, Y_ORDER)].astype(jnp.float32)).astype(LINK)
    for j in range(RING):
        send_ref[Z_ORDER.index(j)] = jnp.where(j > z, both, alone)


def convolve_project(
    came_ref, ends_ref, x_ref, query_ref, residue_ref, rate_ref, weight_ref,
    send_ref, gated_ref, y_ref,
):
    core = lax.rem(lax.axis_index("tensor"), 2)
    z = lax.rem(lax.axis_index("context"), RING)
    shrink = jnp.exp(-rate_ref[...] * (ROWS / SEQ))
    carry = jnp.zeros((POLES, CHANNELS), jnp.float32)
    for j in range(RING):
        came = came_ref[place_of(lax.rem(z + j, RING), Z_ORDER)].astype(jnp.float32)
        carry = carry * shrink + came
    for g, lanes in enumerate(GROUPS):
        rate = rate_ref[:, lanes] / SEQ
        steps = over_subs(rate)
        shrink_sub = jnp.exp(-steps * STEPS)
        sub = sub_index()
        state = jnp.where(sub > 0, pltpu.roll(ends_ref[:, :, lanes], 1, 1), over_subs(carry[:, lanes]))
        for shift in (1, 2, 4):
            state = state + jnp.where(sub >= shift, pltpu.roll(state, shift, 1), 0.0) * shrink_sub
            shrink_sub = shrink_sub * shrink_sub
        shrink_one = over_subs(jnp.exp(-rate))
        residue = over_subs(residue_ref[:, lanes])
        for t in range(STEPS):
            row = x_ref[g, pl.ds(t, SUBS, stride=STEPS), :]
            state = shrink_one * state + row[None]
            y_ref[g, pl.ds(t, SUBS, stride=STEPS), :] = jnp.sum(residue * state, axis=0)
    convolved = jnp.concatenate([y_ref[g] for g in range(len(GROUPS))], axis=1)
    gated = (query_ref[...].astype(jnp.float32) * convolved).astype(jnp.bfloat16)
    gated_ref[...] = gated
    project(gated, weight_ref, 1 - core, send_ref)


def project(gated, weight_ref, core, out_ref):
    for place, chip in enumerate(X_ORDER):
        column = pl.multiple_of((2 * chip + core) * CHANNELS, CHANNELS)
        partial = jnp.dot(
            gated, weight_ref[:, pl.ds(column, CHANNELS)], preferred_element_type=jnp.float32
        )
        out_ref[place] = partial.astype(out_ref.dtype)


def project_own(gated_ref, weight_ref, keep_ref):
    project(gated_ref[...], weight_ref, lax.rem(lax.axis_index("tensor"), 2), keep_ref)


def add_pair(kept_ref, came_ref, out_ref):
    total = kept_ref[...].astype(jnp.float32) + came_ref[...].astype(jnp.float32)
    out_ref[...] = total.astype(out_ref.dtype)


def add_chips(came_ref, out_ref):
    total = came_ref[0].astype(jnp.float32)
    for chip in range(1, XCHIPS):
        total = total + came_ref[chip].astype(jnp.float32)
    out_ref[...] = total.astype(out_ref.dtype)


def kernel(body, outs, scratch=(), flops=0, moved=0, **specs):
    return pl.pallas_call(
        body,
        **specs,
        out_shape=[jax.ShapeDtypeStruct(shape, dtype) for shape, dtype in outs],
        scratch_shapes=scratch,
        compiler_params=pltpu.CompilerParams(vmem_limit_bytes=32 * 2**20),
        cost_estimate=pl.CostEstimate(flops=flops, bytes_accessed=moved, transcendentals=0),
    )


def on_device(queries, key_gate, values, residues, decay_rates, out_weight):
    f32, bf16 = jnp.float32, jnp.bfloat16
    block = (RING, POLES, CHANNELS)
    rows, modes = (ROWS, CHANNELS), (POLES, CHANNELS)
    x, ends, sent = kernel(
        end_states,
        [((len(GROUPS), ROWS, LANES), f32), ((POLES, SUBS, CHANNELS), f32), (block, LINK)],
        scratch=[
            pltpu.VMEM(rows, bf16),
            pltpu.VMEM(rows, bf16),
            pltpu.VMEM(modes, f32),
            pltpu.SemaphoreType.DMA((3,)),
        ],
        in_specs=[pl.BlockSpec(memory_space=pltpu.HBM)] * 3,
        flops=8_000_000_000, moved=1_000_000,
    )(*(pltpu.with_memory_space_constraint(a, pltpu.HBM) for a in (key_gate, values, decay_rates)))
    came = lax.all_to_all(sent, "context", 0, 0, axis_index_groups=Y_GROUPS)
    (sent,) = kernel(row_carry, [(block, LINK)], flops=8_000_000_000, moved=300_000)(
        came, decay_rates
    )
    came = lax.all_to_all(sent, "context", 0, 0, axis_index_groups=Z_GROUPS)
    halves = (XCHIPS, ROWS, CHANNELS)
    sent, gated = kernel(
        convolve_project,
        [(halves, bf16), (rows, bf16)],
        scratch=[pltpu.VMEM((len(GROUPS), ROWS, LANES), f32)],
        flops=300_000_000, moved=3_000_000,
    )(came, ends, x, queries, residues, decay_rates, out_weight)
    came = lax.ppermute(sent, "tensor", SIBLING)
    (kept,) = kernel(project_own, [(halves, f32)], flops=600_000_000, moved=3_000_000)(
        gated, out_weight
    )
    (pair,) = kernel(add_pair, [(halves, bf16)], flops=300_000, moved=1_500_000)(kept, came)
    came = lax.all_to_all(pair, "tensor", 0, 0, axis_index_groups=X_GROUPS)
    (mixed,) = kernel(add_chips, [(rows, bf16)], flops=300_000, moved=700_000)(came)
    return mixed


def solution(mesh):
    in_specs = (
        P("context", "tensor"),
        P("context", "tensor"),
        P("context", "tensor"),
        P(None, "tensor"),
        P(None, "tensor"),
        P("tensor", None),
    )
    out_specs = P("context", "tensor")
    return jax.shard_map(
        on_device, mesh=mesh, in_specs=in_specs, out_specs=out_specs, check_vma=False
    )
```

```python
import jax
import jax.numpy as jnp
from jax import lax
from jax.experimental import pallas as pl
from jax.experimental.pallas import tpu as pltpu
from jax.sharding import PartitionSpec as P

SEQ = 8192
POLES = 16
ROWS = 128
CHANNELS = 512
LANES = 128
SUBS = 8
STEPS = ROWS // SUBS
RING = 8
XCHIPS = 4
LINK = jnp.bfloat16

GROUPS = tuple(slice(g * LANES, (g + 1) * LANES) for g in range(CHANNELS // LANES))
Y_ORDER = (4, 0, 6, 2, 5, 1, 7, 3)
Z_ORDER = (7, 3, 5, 1, 6, 2, 4, 0)
X_ORDER = (3, 1, 2, 0)
Z_GROUPS = [[y * RING + z for z in Z_ORDER] for y in range(RING)]
Y_GROUPS = [[y * RING + z for y in Y_ORDER] for z in range(RING)]
X_GROUPS = [[x * 2 + core for x in X_ORDER] for core in range(2)]
SIBLING = [(t, t ^ 1) for t in range(2 * XCHIPS)]


def over_subs(rows):
    return jnp.broadcast_to(rows[:, None, :], (POLES, SUBS, LANES))


def sub_index():
    return lax.broadcasted_iota(jnp.int32, (POLES, SUBS, LANES), 1).astype(jnp.float32)


def end_states(
    gate_hbm, value_hbm, rate_hbm, x_ref, ends_ref, send_ref, gate_ref, value_ref, rate_ref, sems
):
    pairs = ((gate_hbm, gate_ref), (value_hbm, value_ref), (rate_hbm, rate_ref))
    copies = [pltpu.make_async_copy(a, b, sems.at[i]) for i, (a, b) in enumerate(pairs)]
    for copy in copies:
        copy.start()
    for copy in copies:
        copy.wait()
    product = gate_ref[...].astype(jnp.float32) * value_ref[...].astype(jnp.float32)
    product = product.astype(jnp.bfloat16).astype(jnp.float32)
    for g, lanes in enumerate(GROUPS):
        x_ref[g] = product[:, lanes]
        rate = rate_ref[:, lanes] / SEQ
        shrink = over_subs(jnp.exp(-rate))
        state = jnp.zeros((POLES, SUBS, LANES), jnp.float32)
        for t in range(STEPS):
            row = x_ref[g, pl.ds(t, SUBS, stride=STEPS), :]
            state = shrink * state + row[None]
        ends_ref[:, :, lanes] = state
        left = STEPS * (SUBS - 1.0 - sub_index())
        total = jnp.sum(state * jnp.exp(-over_subs(rate) * left), axis=1).astype(LINK)
        for j in range(RING):
            send_ref[j, :, lanes] = total


def chunk_carry(came_ref, rate_ref, prior_ref, send_ref):
    z = lax.rem(lax.axis_index("context"), RING)
    shrink = jnp.exp(-rate_ref[...] * (ROWS / SEQ))
    prior = jnp.zeros((POLES, CHANNELS), jnp.float32)
    total = jnp.zeros((POLES, CHANNELS), jnp.float32)
    for j in range(RING):
        came = came_ref[Z_ORDER.index(j)].astype(jnp.float32)
        prior = jnp.where(j < z, prior * shrink + came, prior)
        total = total * shrink + came
    prior_ref[...] = prior
    sent = total.astype(LINK)
    for j in range(RING):
        send_ref[j] = sent


def convolve_project(
    came_ref, prior_ref, ends_ref, x_ref, query_ref, residue_ref, rate_ref, weight_ref,
    send_ref, gated_ref, y_ref,
):
    context = lax.axis_index("context")
    core = lax.rem(lax.axis_index("tensor"), 2)
    z, y = lax.rem(context, RING), context // RING
    shrink = jnp.exp(-rate_ref[...] * (RING * ROWS / SEQ))
    carry = jnp.zeros((POLES, CHANNELS), jnp.float32)
    for j in range(RING):
        carry = jnp.where(j < y, carry * shrink + came_ref[Y_ORDER.index(j)].astype(jnp.float32), carry)
    behind = (z * ROWS).astype(jnp.float32) / SEQ
    carry = carry * jnp.exp(-rate_ref[...] * behind) + prior_ref[...]
    for g, lanes in enumerate(GROUPS):
        rate = rate_ref[:, lanes] / SEQ
        steps = over_subs(rate)
        shrink_sub = jnp.exp(-steps * STEPS)
        sub = sub_index()
        state = jnp.where(sub > 0, pltpu.roll(ends_ref[:, :, lanes], 1, 1), over_subs(carry[:, lanes]))
        for shift in (1, 2, 4):
            state = state + jnp.where(sub >= shift, pltpu.roll(state, shift, 1), 0.0) * shrink_sub
            shrink_sub = shrink_sub * shrink_sub
        shrink_one = over_subs(jnp.exp(-rate))
        residue = over_subs(residue_ref[:, lanes])
        for t in range(STEPS):
            row = x_ref[g, pl.ds(t, SUBS, stride=STEPS), :]
            state = shrink_one * state + row[None]
            y_ref[g, pl.ds(t, SUBS, stride=STEPS), :] = jnp.sum(residue * state, axis=0)
    convolved = jnp.concatenate([y_ref[g] for g in range(len(GROUPS))], axis=1)
    gated = (query_ref[...].astype(jnp.float32) * convolved).astype(jnp.bfloat16)
    gated_ref[...] = gated
    project(gated, weight_ref, 1 - core, send_ref)


def project(gated, weight_ref, core, out_ref):
    for place, chip in enumerate(X_ORDER):
        column = pl.multiple_of((2 * chip + core) * CHANNELS, CHANNELS)
        partial = jnp.dot(
            gated, weight_ref[:, pl.ds(column, CHANNELS)], preferred_element_type=jnp.float32
        )
        out_ref[place] = partial.astype(out_ref.dtype)


def project_own(gated_ref, weight_ref, keep_ref):
    project(gated_ref[...], weight_ref, lax.rem(lax.axis_index("tensor"), 2), keep_ref)


def add_pair(kept_ref, came_ref, out_ref):
    total = kept_ref[...].astype(jnp.float32) + came_ref[...].astype(jnp.float32)
    out_ref[...] = total.astype(out_ref.dtype)


def add_chips(came_ref, out_ref):
    total = came_ref[0].astype(jnp.float32)
    for chip in range(1, XCHIPS):
        total = total + came_ref[chip].astype(jnp.float32)
    out_ref[...] = total.astype(out_ref.dtype)


def kernel(body, outs, scratch=(), flops=0, moved=0, **specs):
    return pl.pallas_call(
        body,
        **specs,
        out_shape=[jax.ShapeDtypeStruct(shape, dtype) for shape, dtype in outs],
        scratch_shapes=scratch,
        compiler_params=pltpu.CompilerParams(vmem_limit_bytes=32 * 2**20),
        cost_estimate=pl.CostEstimate(flops=flops, bytes_accessed=moved, transcendentals=0),
    )


def on_device(queries, key_gate, values, residues, decay_rates, out_weight):
    f32, bf16 = jnp.float32, jnp.bfloat16
    block = (RING, POLES, CHANNELS)
    rows, modes = (ROWS, CHANNELS), (POLES, CHANNELS)
    x, ends, sent = kernel(
        end_states,
        [((len(GROUPS), ROWS, LANES), f32), ((POLES, SUBS, CHANNELS), f32), (block, LINK)],
        scratch=[
            pltpu.VMEM(rows, bf16),
            pltpu.VMEM(rows, bf16),
            pltpu.VMEM(modes, f32),
            pltpu.SemaphoreType.DMA((3,)),
        ],
        in_specs=[pl.BlockSpec(memory_space=pltpu.HBM)] * 3,
        flops=8_000_000_000, moved=1_000_000,
    )(*(pltpu.with_memory_space_constraint(a, pltpu.HBM) for a in (key_gate, values, decay_rates)))
    came = lax.all_to_all(sent, "context", 0, 0, axis_index_groups=Z_GROUPS)
    prior, sent = kernel(
        chunk_carry, [(modes, f32), (block, LINK)], flops=8_000_000_000, moved=300_000
    )(came, decay_rates)
    came = lax.all_to_all(sent, "context", 0, 0, axis_index_groups=Y_GROUPS)
    halves = (XCHIPS, ROWS, CHANNELS)
    sent, gated = kernel(
        convolve_project,
        [(halves, bf16), (rows, bf16)],
        scratch=[pltpu.VMEM((len(GROUPS), ROWS, LANES), f32)],
        flops=300_000_000, moved=3_000_000,
    )(came, prior, ends, x, queries, residues, decay_rates, out_weight)
    came = lax.ppermute(sent, "tensor", SIBLING)
    (kept,) = kernel(project_own, [(halves, f32)], flops=600_000_000, moved=3_000_000)(
        gated, out_weight
    )
    (pair,) = kernel(add_pair, [(halves, bf16)], flops=300_000, moved=1_500_000)(kept, came)
    came = lax.all_to_all(pair, "tensor", 0, 0, axis_index_groups=X_GROUPS)
    (mixed,) = kernel(add_chips, [(rows, bf16)], flops=300_000, moved=700_000)(came)
    return mixed


def solution(mesh):
    in_specs = (
        P("context", "tensor"),
        P("context", "tensor"),
        P("context", "tensor"),
        P(None, "tensor"),
        P(None, "tensor"),
        P("tensor", None),
    )
    out_specs = P("context", "tensor")
    return jax.shard_map(
        on_device, mesh=mesh, in_specs=in_specs, out_specs=out_specs, check_vma=False
    )
```

```python
import jax
import jax.numpy as jnp
from jax import lax
from jax.experimental import pallas as pl
from jax.experimental.pallas import tpu as pltpu
from jax.sharding import PartitionSpec as P

SEQ = 8192
POLES = 16
ROWS = 128
CHANNELS = 512
LANES = 128
SUBS = 8
STEPS = ROWS // SUBS
RING = 8
XCHIPS = 4
LINK = jnp.bfloat16

GROUPS = tuple(slice(g * LANES, (g + 1) * LANES) for g in range(CHANNELS // LANES))
Y_ORDER = (4, 0, 6, 2, 5, 1, 7, 3)
Z_ORDER = (7, 3, 5, 1, 6, 2, 4, 0)
X_ORDER = (3, 1, 2, 0)
Z_GROUPS = [[y * RING + z for z in Z_ORDER] for y in range(RING)]
Y_GROUPS = [[y * RING + z for y in Y_ORDER] for z in range(RING)]
X_GROUPS = [[x * 2 + core for x in X_ORDER] for core in range(2)]
SIBLING = [(t, t ^ 1) for t in range(2 * XCHIPS)]


def over_subs(rows):
    return jnp.broadcast_to(rows[:, None, :], (POLES, SUBS, LANES))


def end_states(
    gate_hbm, value_hbm, rate_hbm, x_ref, before_ref, fade_ref, send_ref,
    gate_ref, value_ref, rate_ref, sems,
):
    pairs = ((gate_hbm, gate_ref), (value_hbm, value_ref), (rate_hbm, rate_ref))
    copies = [pltpu.make_async_copy(a, b, sems.at[i]) for i, (a, b) in enumerate(pairs)]
    for copy in copies:
        copy.start()
    for copy in copies:
        copy.wait()
    product = gate_ref[...].astype(jnp.float32) * value_ref[...].astype(jnp.float32)
    product = product.astype(jnp.bfloat16).astype(jnp.float32)
    for g, lanes in enumerate(GROUPS):
        x_ref[g] = product[:, lanes]
        rate = rate_ref[:, lanes] / SEQ
        shrink = over_subs(jnp.exp(-rate))
        state = jnp.zeros((POLES, SUBS, LANES), jnp.float32)
        for t in range(STEPS):
            row = x_ref[g, pl.ds(t, SUBS, stride=STEPS), :]
            state = shrink * state + row[None]
        shrink = over_subs(jnp.exp(-rate * STEPS))
        fade = jnp.ones_like(state)
        sub = lax.broadcasted_iota(jnp.int32, state.shape, 1)
        for shift in (1, 2, 4):
            later = sub >= shift
            state = state + pltpu.roll(state, shift, 1) * jnp.where(later, shrink, 0.0)
            fade = fade * jnp.where((sub & shift) > 0, shrink, 1.0)
            shrink = shrink * shrink
        before_ref[:, :, lanes] = jnp.where(sub > 0, pltpu.roll(state, 1, 1), 0.0)
        fade_ref[:, :, lanes] = fade
        total = state[:, SUBS - 1, :].astype(LINK)
        for j in range(RING):
            send_ref[j, :, lanes] = total


def chunk_carry(came_ref, rate_ref, prior_ref, send_ref):
    z = lax.rem(lax.axis_index("context"), RING)
    shrink = jnp.exp(-rate_ref[...] * (ROWS / SEQ))
    prior = jnp.zeros((POLES, CHANNELS), jnp.float32)
    total = jnp.zeros((POLES, CHANNELS), jnp.float32)
    for j in range(RING):
        came = came_ref[Z_ORDER.index(j)].astype(jnp.float32)
        prior = jnp.where(j < z, prior * shrink + came, prior)
        total = total * shrink + came
    prior_ref[...] = prior
    sent = total.astype(LINK)
    for j in range(RING):
        send_ref[j] = sent


def convolve_project(
    came_ref, prior_ref, before_ref, fade_ref, x_ref, query_ref, residue_ref, rate_ref, weight_ref,
    send_ref, gated_ref, y_ref,
):
    context = lax.axis_index("context")
    core = lax.rem(lax.axis_index("tensor"), 2)
    z, y = lax.rem(context, RING), context // RING
    shrink = jnp.exp(-rate_ref[...] * (RING * ROWS / SEQ))
    carry = jnp.zeros((POLES, CHANNELS), jnp.float32)
    for j in range(RING):
        carry = jnp.where(j < y, carry * shrink + came_ref[Y_ORDER.index(j)].astype(jnp.float32), carry)
    behind = (z * ROWS).astype(jnp.float32) / SEQ
    carry = carry * jnp.exp(-rate_ref[...] * behind) + prior_ref[...]
    for g, lanes in enumerate(GROUPS):
        state = before_ref[:, :, lanes] + over_subs(carry[:, lanes]) * fade_ref[:, :, lanes]
        shrink_one = over_subs(jnp.exp(-rate_ref[:, lanes] / SEQ))
        residue = over_subs(residue_ref[:, lanes])
        for t in range(STEPS):
            row = x_ref[g, pl.ds(t, SUBS, stride=STEPS), :]
            state = shrink_one * state + row[None]
            y_ref[g, pl.ds(t, SUBS, stride=STEPS), :] = jnp.sum(residue * state, axis=0)
    convolved = jnp.concatenate([y_ref[g] for g in range(len(GROUPS))], axis=1)
    gated = (query_ref[...].astype(jnp.float32) * convolved).astype(jnp.bfloat16)
    gated_ref[...] = gated
    project(gated, weight_ref, 1 - core, send_ref)


def project(gated, weight_ref, core, out_ref):
    for place, chip in enumerate(X_ORDER):
        column = pl.multiple_of((2 * chip + core) * CHANNELS, CHANNELS)
        partial = jnp.dot(
            gated, weight_ref[:, pl.ds(column, CHANNELS)], preferred_element_type=jnp.float32
        )
        out_ref[place] = partial.astype(out_ref.dtype)


def project_own(gated_ref, weight_ref, keep_ref):
    project(gated_ref[...], weight_ref, lax.rem(lax.axis_index("tensor"), 2), keep_ref)


def add_pair(kept_ref, came_ref, out_ref):
    total = kept_ref[...].astype(jnp.float32) + came_ref[...].astype(jnp.float32)
    out_ref[...] = total.astype(out_ref.dtype)


def add_chips(came_ref, out_ref):
    total = came_ref[0].astype(jnp.float32)
    for chip in range(1, XCHIPS):
        total = total + came_ref[chip].astype(jnp.float32)
    out_ref[...] = total.astype(out_ref.dtype)


def kernel(body, outs, scratch=(), flops=0, moved=0, **specs):
    return pl.pallas_call(
        body,
        **specs,
        out_shape=[jax.ShapeDtypeStruct(shape, dtype) for shape, dtype in outs],
        scratch_shapes=scratch,
        compiler_params=pltpu.CompilerParams(vmem_limit_bytes=32 * 2**20),
        cost_estimate=pl.CostEstimate(flops=flops, bytes_accessed=moved, transcendentals=0),
    )


def on_device(queries, key_gate, values, residues, decay_rates, out_weight):
    f32, bf16 = jnp.float32, jnp.bfloat16
    block = (RING, POLES, CHANNELS)
    rows, modes, subs = (ROWS, CHANNELS), (POLES, CHANNELS), (POLES, SUBS, CHANNELS)
    x, before, fade, sent = kernel(
        end_states,
        [((len(GROUPS), ROWS, LANES), f32), (subs, f32), (subs, f32), (block, LINK)],
        scratch=[
            pltpu.VMEM(rows, bf16),
            pltpu.VMEM(rows, bf16),
            pltpu.VMEM(modes, f32),
            pltpu.SemaphoreType.DMA((3,)),
        ],
        in_specs=[pl.BlockSpec(memory_space=pltpu.HBM)] * 3,
        flops=8_000_000_000, moved=1_000_000,
    )(*(pltpu.with_memory_space_constraint(a, pltpu.HBM) for a in (key_gate, values, decay_rates)))
    came = lax.all_to_all(sent, "context", 0, 0, axis_index_groups=Z_GROUPS)
    prior, sent = kernel(
        chunk_carry, [(modes, f32), (block, LINK)], flops=8_000_000_000, moved=300_000
    )(came, decay_rates)
    came = lax.all_to_all(sent, "context", 0, 0, axis_index_groups=Y_GROUPS)
    halves = (XCHIPS, ROWS, CHANNELS)
    sent, gated = kernel(
        convolve_project,
        [(halves, bf16), (rows, bf16)],
        scratch=[pltpu.VMEM((len(GROUPS), ROWS, LANES), f32)],
        flops=300_000_000, moved=3_000_000,
    )(came, prior, before, fade, x, queries, residues, decay_rates, out_weight)
    came = lax.ppermute(sent, "tensor", SIBLING)
    (kept,) = kernel(project_own, [(halves, f32)], flops=600_000_000, moved=3_000_000)(
        gated, out_weight
    )
    (pair,) = kernel(add_pair, [(halves, bf16)], flops=300_000, moved=1_500_000)(kept, came)
    came = lax.all_to_all(pair, "tensor", 0, 0, axis_index_groups=X_GROUPS)
    (mixed,) = kernel(add_chips, [(rows, bf16)], flops=300_000, moved=700_000)(came)
    return mixed


def solution(mesh):
    in_specs = (
        P("context", "tensor"),
        P("context", "tensor"),
        P("context", "tensor"),
        P(None, "tensor"),
        P(None, "tensor"),
        P("tensor", None),
    )
    out_specs = P("context", "tensor")
    return jax.shard_map(
        on_device, mesh=mesh, in_specs=in_specs, out_specs=out_specs, check_vma=False
    )
```
